128 devices in a mesh: inst: 16 (over z_hi, y, core), tp: 8 (over x, z_lo).
Axes of the slice: x: 4, y: 4, z: 4 (z_hi: 2, z_lo: 2; z = z_hi * 2 + z_lo), core: 2. Of those that a mesh axis runs over, the one named last changes fastest.
Arguments:
- q_prefill: bfloat16 [16384, 4096], P('inst', 'tp'), may hold values from -70 to 70
- k_prefill: bfloat16 [16384, 1024], P('inst', 'tp'), may hold values from -6 to 6
- v_prefill: bfloat16 [16384, 1024], P('inst', 'tp'), may hold values from -6 to 6
- q_decode: bfloat16 [2, 128, 4096], P(None, 'inst', 'tp'), may hold values from -70 to 70
- k_new: bfloat16 [2, 128, 1024], P(None, 'inst', 'tp'), may hold values from -6 to 6
- v_new: bfloat16 [2, 128, 1024], P(None, 'inst', 'tp'), may hold values from -6 to 6
- k_cache: bfloat16 [2048, 128, 1024], P('inst', None, 'tp'), may hold values from -6 to 6
- v_cache: bfloat16 [2048, 128, 1024], P('inst', None, 'tp'), may hold values from -6 to 6
- block_table: int32 [128, 16], replicated, may hold values from 0 to 2047, as said below
- req_lengths: int32 [128], replicated, may hold values from 1 to 2048, 157286 in all
Outputs:
- prefill_out: bfloat16 [16384, 4096], P('inst', 'tp')
- decode_out: bfloat16 [2, 128, 4096], P(None, 'inst', 'tp')
The draws below stay inside these ranges and needn't reach their ends.
Inputs may be any that keep to these rules, and one draw needn't show every extreme that they name: `block_table`: each block number appears exactly once in the table.
All inputs are finite; a program needn't handle non-finite values.
Results may differ from the reference program's by a relative error of at most 0.009.
Values may be sent and summed in bfloat16 or wider, within the bound.
No kernel may reach another device: no remote copies, remote signals or barrier semaphores. Data moves between devices by JAX's collectives and lax.ppermute only.
A program may use at most 128 MiB of HBM per device.

```python
import math
import jax
import jax.numpy as jnp
import numpy as np
from jax import lax

H = 32
KVH = 8
HD = 128
TOK_DEV = 1024
MAXB = 16
BLOCK = 128
STEPS = 2
TOKENS = 16384
R = 128
NBLK = 2048


def drawn_rows(key, row_count, col_count):
    return jnp.clip(jax.random.normal(key, (row_count, col_count), jnp.float32), -6.0, 6.0)


def draw_q_prefill(key, part):
    key = jax.random.fold_in(key, 11)
    values = drawn_rows(key, TOKENS, H * HD)
    return values.astype(jnp.bfloat16)


def draw_q_decode(key, part):
    key = jax.random.fold_in(key, 23)
    values = drawn_rows(key, STEPS * R, H * HD)
    return values.reshape(STEPS, R, H * HD).astype(jnp.bfloat16)


def draw_block_table(key, part):
    key = jax.random.fold_in(key, 37)
    order = jax.random.permutation(key, R * MAXB).astype(jnp.int32)
    return order.reshape(R, MAXB)


def block_scale(key, extent, pieces, low, largest):
    gain = 1.0
    for axis_at, shards_of in pieces:
        heights = jax.random.uniform(jax.random.fold_in(jax.random.fold_in(key, 6), axis_at), (shards_of,), jnp.float32, low / len(pieces), largest / len(pieces))
        gain = gain * jnp.repeat(jnp.exp(heights), extent[axis_at] // shards_of).reshape((-1,) + (1,) * (len(extent) - 1 - axis_at))
    return gain


def length_profile(count, total, bound, skew):
    weights = [(1 << 20) // math.isqrt(rank ** skew) + 1 for rank in range(2, count + 1)]
    surplus, counts = total - bound - (count - 1), [1] * (count - 1)
    while surplus > 0:
        movable = [i for i in range(count - 1) if counts[i] < bound]
        whole, remaining = sum([weights[i] for i in movable]), surplus
        for i in movable:
            addition = min(bound - counts[i], max(1, remaining * weights[i] // whole), surplus)
            counts[i] = counts[i] + addition
            surplus = surplus - addition
    return np.array([bound] + counts)


def uneven_parts(stream_key, number_of, total, reach, slope):
    if number_of == 2:
        one = jax.random.randint(stream_key, (), max(1, total - reach), min(reach, total - 1) + 1)
        return jnp.stack([one, total - one])
    lengths = jnp.asarray(length_profile(number_of, total, reach, slope), jnp.int32)
    couples = (number_of - 1) // 2
    giver, sink = lengths[1:1 + 2 * couples:2], lengths[2:2 + 2 * couples:2]
    room = jnp.minimum(giver - 1, reach - sink)
    moved = jax.random.randint(jax.random.fold_in(stream_key, 1), (couples,), 0, 1 << 20) % (room + 1)
    lengths = lengths.at[1:1 + 2 * couples:2].set(giver - moved).at[2:2 + 2 * couples:2].set(sink + moved)
    return lengths[jax.random.permutation(jax.random.fold_in(stream_key, 2), number_of)]


def scatter_about(own_key, extent, deviation, reach, pieces=(), kind=jnp.bfloat16):
    factor_of = block_scale(own_key, extent, pieces, -0.22, 0.18) if pieces else 1.0
    values = jax.random.normal(own_key, extent, jnp.float32) * deviation * factor_of
    return jnp.minimum(jnp.maximum(values, -reach), reach).astype(kind)


def setup_inputs(seed: int = 0) -> dict:
    key_of = jax.random.split(jax.random.key(seed), 11)
    return {
        "q_prefill": draw_q_prefill(jax.random.fold_in(key_of[10], 71), 0),
        "k_prefill": scatter_about(key_of[1], (TOKENS, KVH * HD), 1.0, 6.0, ((0, 16), (1, 8))),
        "v_prefill": scatter_about(key_of[2], (TOKENS, KVH * HD), 1.0, 6.0, ((0, 16), (1, 8))),
        "q_decode": draw_q_decode(jax.random.fold_in(key_of[10], 71), 0),
        "k_new": scatter_about(key_of[4], (STEPS, R, KVH * HD), 1.0, 6.0, ((1, 16), (2, 8))),
        "v_new": scatter_about(key_of[5], (STEPS, R, KVH * HD), 1.0, 6.0, ((1, 16), (2, 8))),
        "k_cache": scatter_about(key_of[6], (NBLK, BLOCK, KVH * HD), 1.0, 6.0, ((0, 16), (2, 8))),
        "v_cache": scatter_about(key_of[7], (NBLK, BLOCK, KVH * HD), 1.0, 6.0, ((0, 16), (2, 8))),
        "block_table": draw_block_table(jax.random.fold_in(key_of[10], 71), 0),
        "req_lengths": uneven_parts(key_of[9], R, R * MAXB * BLOCK * 3 // 5, MAXB * BLOCK, 2).astype(jnp.int32),
    }


def prefill_attention(q_prefill, k_prefill, v_prefill):
    group_size = H // KVH
    softmax_scale = HD ** -0.5
    queries = q_prefill.astype(jnp.float32).reshape(TOKENS, KVH, group_size, HD)
    key_all = k_prefill.astype(jnp.float32).reshape(TOKENS, KVH, HD)
    value_all = v_prefill.astype(jnp.float32).reshape(TOKENS, KVH, HD)
    n_blocks = TOKENS // TOK_DEV
    key_pos = jnp.arange(TOKENS, dtype=jnp.int32)

    def block_head(flat_index):
        block_id = flat_index // KVH
        head_id = flat_index % KVH
        first_row = (block_id * TOK_DEV).astype(jnp.int32)
        query_blk = lax.dynamic_slice_in_dim(queries, first_row, TOK_DEV, 0)
        query_blk = lax.dynamic_index_in_dim(query_blk, head_id, 1, keepdims=False)
        key_head = lax.dynamic_index_in_dim(key_all, head_id, 1, keepdims=False)
        value_head = lax.dynamic_index_in_dim(value_all, head_id, 1, keepdims=False)
        scores = jnp.einsum('tgd,sd->tgs', query_blk, key_head) * softmax_scale
        query_pos = first_row + jnp.arange(TOK_DEV, dtype=jnp.int32)
        allowed = key_pos[None, :] <= query_pos[:, None]
        scores = jnp.where(allowed[:, None, :], scores, -1e30)
        highest = jnp.max(scores, axis=-1, keepdims=True)
        weights = jnp.where(allowed[:, None, :], jnp.exp(scores - highest), 0.0)
        total = jnp.sum(weights, axis=-1)
        rounded = weights.astype(jnp.bfloat16).astype(jnp.float32)
        mixed = jnp.einsum('tgs,sd->tgd', rounded, value_head)
        return mixed / total[..., None]

    blocks = lax.map(block_head, jnp.arange(n_blocks * KVH, dtype=jnp.int32))
    blocks = blocks.reshape(n_blocks, KVH, TOK_DEV, group_size, HD).transpose(0, 2, 1, 3, 4)
    return blocks.reshape(TOKENS, H * HD).astype(jnp.bfloat16)


def decode_attention(q_decode, k_new, v_new, k_cache, v_cache, block_table, req_lengths):
    group_size = H // KVH
    softmax_scale = HD ** -0.5
    slot_pos = jnp.arange(MAXB * BLOCK, dtype=jnp.int32)

    def one_request(request):
        table_row = block_table[request]
        key_rows = k_cache[table_row].astype(jnp.float32).reshape(MAXB * BLOCK, KVH, HD)
        value_rows = v_cache[table_row].astype(jnp.float32).reshape(MAXB * BLOCK, KVH, HD)
        live = slot_pos < req_lengths[request]
        results = []
        for step in range(STEPS):
            query = q_decode[step, request].astype(jnp.float32).reshape(KVH, group_size, HD)
            cache_scores = jnp.einsum('kgd,skd->kgs', query, key_rows) * softmax_scale
            cache_scores = jnp.where(live[None, None, :], cache_scores, -1e30)
            new_keys = k_new[:step + 1, request].astype(jnp.float32).reshape(step + 1, KVH, HD)
            new_values = v_new[:step + 1, request].astype(jnp.float32).reshape(step + 1, KVH, HD)
            new_scores = jnp.einsum('kgd,nkd->kgn', query, new_keys) * softmax_scale
            highest = jnp.maximum(jnp.max(cache_scores, axis=-1), jnp.max(new_scores, axis=-1))
            cache_w = jnp.where(live[None, None, :], jnp.exp(cache_scores - highest[..., None]), 0.0)
            new_w = jnp.exp(new_scores - highest[..., None])
            total = jnp.sum(cache_w, axis=-1) + jnp.sum(new_w, axis=-1)
            rounded = cache_w.astype(jnp.bfloat16).astype(jnp.float32)
            mixed = jnp.einsum('kgs,skd->kgd', rounded, value_rows) + jnp.einsum('kgn,nkd->kgd', new_w, new_values)
            results.append((mixed / total[..., None]).reshape(H * HD))
        return jnp.stack(results)

    result = lax.map(one_request, jnp.arange(R, dtype=jnp.int32))
    return result.transpose(1, 0, 2).astype(jnp.bfloat16)


def reference(q_prefill, k_prefill, v_prefill, q_decode, k_new, v_new, k_cache, v_cache, block_table, req_lengths):
    prefill_out = prefill_attention(q_prefill, k_prefill, v_prefill)
    decode_out = decode_attention(q_decode, k_new, v_new, k_cache, v_cache, block_table, req_lengths)
    return (prefill_out, decode_out)
```

```python
import functools
import math

import jax
import jax.numpy as jnp
from jax import lax
from jax.experimental import pallas as pl
from jax.experimental.pallas import tpu as pltpu
from jax.sharding import PartitionSpec as P

HD = 128
SCALE2 = HD**-0.5 * math.log2(math.e)
LOW = -1e30
HEADS = 4
ROWS = 512
KEYS = 1024
CHUNK = 256
SLOTS = 8
VMEM = pl.BlockSpec(memory_space=pltpu.VMEM)
SMEM = pl.BlockSpec(memory_space=pltpu.SMEM)
ANY = pl.BlockSpec(memory_space=pl.ANY)
NT = (((1,), (1,)), ((), ()))


def index_of(z, y, c):
    return (z % 2) * 8 + (y % 4) * 2 + c % 2


def moves(dz, dy, dc):
    return [
        (index_of(z, y, c), index_of(z + dz, y + dy, c + dc))
        for z in range(2)
        for y in range(4)
        for c in range(2)
    ]


def permute(value, pairs):
    return lax.ppermute(value, "inst", pairs)


def flash_kernel(half_count, sources, has_state, final, diag, *refs):
    refs = list(refs)
    meta, q_ref = refs.pop(0), refs.pop(0)
    kv_refs = [refs.pop(0) for _ in range(1 + max(src for src, *_ in sources))]
    state_in = [refs.pop(0) for _ in range(2)] if has_state else None
    outs = [refs.pop(0) for _ in range(1 if final else 2)]
    kv, qs, acc, top, scores, row_top, items, sem = refs

    copies = [
        pltpu.make_async_copy(
            kv_refs[src].at[pl.ds(first, count)],
            kv.at[slot, pl.ds(row, count)],
            sem.at[k],
        )
        for k, (src, first, count, slot, row) in enumerate(sources)
    ]
    for copy in copies:
        copy.start()

    for half in range(half_count):
        for h in range(HEADS):
            scaled = q_ref[half, :, h * HD : (h + 1) * HD].astype(jnp.float32) * SCALE2
            high = scaled.astype(jnp.bfloat16)
            qs[half, h, :, :HD] = high
            qs[half, h, :, HD:] = (scaled - high.astype(jnp.float32)).astype(jnp.bfloat16)
    if has_state:
        lane = lax.broadcasted_iota(jnp.int32, (ROWS, HD), 1)
        for half in range(half_count):
            for h in range(HEADS):
                acc[half, h, :, :HD] = state_in[0][half, h]
                stat = state_in[1][half, h]
                top[half, h] = jnp.broadcast_to(stat[:, :1], (ROWS, HD))
                acc[half, h, :, HD:] = jnp.broadcast_to(stat[:, HD - 1 :], (ROWS, HD))
    else:
        acc[...] = jnp.zeros_like(acc)
        top[...] = jnp.full_like(top, LOW)

    count = jnp.int32(0)
    for half in range(half_count):
        limit = meta[SLOTS + half]
        for slot in range(SLOTS):
            wanted = meta[slot] < limit

            @pl.when(wanted)
            def _(count=count, half=half, slot=slot):
                items[count] = half * SLOTS + slot

            count = count + wanted.astype(jnp.int32)

    for copy in copies:
        copy.wait()

    ones = jnp.ones((KEYS, HD), jnp.bfloat16)

    def update(half, h, row, s, new_top, values):
        old_top = top[half, h, pl.ds(row, CHUNK), :]
        new_top = jnp.maximum(old_top, new_top)
        factor = jnp.exp2(old_top - new_top)
        weights = jnp.exp2(s - new_top[:, :1])
        top[half, h, pl.ds(row, CHUNK), :] = new_top
        mixed = jnp.dot(
            weights.astype(jnp.bfloat16),
            jnp.concatenate([values, ones[: values.shape[0]]], axis=1),
            preferred_element_type=jnp.float32,
        )
        for part in range(2):
            cols = slice(part * HD, (part + 1) * HD)
            acc[half, h, pl.ds(row, CHUNK), cols] = (
                acc[half, h, pl.ds(row, CHUNK), cols] * factor + mixed[:, cols]
            )

    if diag is not None:
        half, first_row = diag
        slot = meta[SLOTS + half_count]
        for r in range(ROWS // CHUNK):
            seen = first_row + (r + 1) * CHUNK
            key_rows = kv[slot, :seen, :HD]
            key_rows = jnp.concatenate([key_rows, key_rows], axis=1)
            row_pos = lax.broadcasted_iota(jnp.int32, (CHUNK, seen), 0) + (seen - CHUNK)
            allowed = lax.broadcasted_iota(jnp.int32, (CHUNK, seen), 1) <= row_pos
            for h in range(HEADS):
                s = lax.dot_general(
                    qs[half, h, r * CHUNK : (r + 1) * CHUNK, :],
                    key_rows,
                    NT,
                    preferred_element_type=jnp.float32,
                )
                s = jnp.where(allowed, s, LOW)
                update(
                    half, h, r * CHUNK, s, jnp.max(s, axis=-1, keepdims=True), kv[slot, :seen, HD:]
                )

    def place(item):
        code = items[item]
        return code // SLOTS, code % SLOTS

    def produce(item, r):
        half, slot = place(item)
        key_rows = kv[slot, :, :HD]
        key_rows = jnp.concatenate([key_rows, key_rows], axis=1)
        for h in range(HEADS):
            s = lax.dot_general(
                qs[half, h, r * CHUNK : (r + 1) * CHUNK, :],
                key_rows,
                NT,
                preferred_element_type=jnp.float32,
            )
            scores[r, h] = s
            row_top[r, h] = jnp.broadcast_to(jnp.max(s, axis=-1, keepdims=True), (CHUNK, HD))

    def consume(item, r):
        half, slot = place(item)
        for h in range(HEADS):
            update(half, h, r * CHUNK, scores[r, h], row_top[r, h], kv[slot, :, HD:])

    @pl.when(count > 0)
    def _():
        produce(0, 0)

        @pl.loop(0, count)
        def _(item):
            produce(item, 1)
            consume(item, 0)
            produce(jnp.minimum(item + 1, count - 1), 0)
            consume(item, 1)

    for half in range(half_count):
        for h in range(HEADS):
            if final:
                outs[0][half, :, h * HD : (h + 1) * HD] = (
                    acc[half, h, :, :HD] / acc[half, h, :, HD:]
                ).astype(jnp.bfloat16)
            else:
                lane = lax.broadcasted_iota(jnp.int32, (ROWS, HD), 1)
                outs[0][half, h] = acc[half, h, :, :HD]
                outs[1][half, h] = jnp.where(lane < HD // 2, top[half, h], acc[half, h, :, HD:])


def flash(meta, queries, kv_arrays, sources, state=None, final=False, diag=None):
    half_count = queries.shape[0]
    if final:
        out_shape = [jax.ShapeDtypeStruct((half_count, ROWS, HEADS * HD), jnp.bfloat16)]
    else:
        out_shape = [jax.ShapeDtypeStruct((half_count, HEADS, ROWS, HD), jnp.float32)] * 2
    operands = [meta, queries, *kv_arrays, *(state or [])]
    in_specs = [SMEM, VMEM] + [ANY] * len(kv_arrays) + [VMEM] * (2 if state else 0)
    work = half_count * SLOTS * HEADS * ROWS * KEYS // 2
    return pl.pallas_call(
        functools.partial(flash_kernel, half_count, sources, state is not None, final, diag),
        out_shape=out_shape,
        in_specs=in_specs,
        out_specs=[VMEM] * len(out_shape),
        scratch_shapes=[
            pltpu.VMEM((SLOTS, KEYS, 2 * HD), jnp.bfloat16),
            pltpu.VMEM((half_count, HEADS, ROWS, 2 * HD), jnp.bfloat16),
            pltpu.VMEM((half_count, HEADS, ROWS, 2 * HD), jnp.float32),
            pltpu.VMEM((half_count, HEADS, ROWS, HD), jnp.float32),
            pltpu.VMEM((2, HEADS, CHUNK, KEYS), jnp.float32),
            pltpu.VMEM((2, HEADS, CHUNK, HD), jnp.float32),
            pltpu.SMEM((2 * SLOTS,), jnp.int32),
            pltpu.SemaphoreType.DMA((len(sources),)),
        ],
        compiler_params=pltpu.CompilerParams(vmem_limit_bytes=48 << 20),
        cost_estimate=pl.CostEstimate(
            flops=work * HD * 4 * 2, bytes_accessed=16 << 20, transcendentals=work
        ),
    )(*operands)


GROUP = 16
QROWS = 8


def decode_kernel(owner, live, q_ref, k_ref, v_ref, out_ref, spread, top, total, mixed):
    step = pl.program_id(0)

    @pl.when(step == 0)
    def _():
        spread[...] = jnp.zeros_like(spread)
        top[...] = jnp.full_like(top, LOW)
        total[...] = jnp.zeros_like(total)
        mixed[...] = jnp.zeros_like(mixed)

    zero = jnp.zeros((QROWS, HD), jnp.float32)
    reqs = [owner[step * GROUP + b] for b in range(GROUP)]
    for b in range(0, GROUP, 2):
        pair = jnp.concatenate(
            [
                jnp.concatenate([q_ref[reqs[b]], zero], axis=1),
                jnp.concatenate([zero, q_ref[reqs[b + 1]]], axis=1),
            ],
            axis=0,
        )
        spread[b * QROWS : (b + 2) * QROWS, b * HD : (b + 2) * HD] = pair.astype(jnp.bfloat16)
    keys = jnp.concatenate([k_ref[b] for b in range(GROUP)], axis=1)
    values = jnp.concatenate([v_ref[b] for b in range(GROUP)], axis=1)
    scores = lax.dot_general(spread[...], keys, NT, preferred_element_type=jnp.float32) * SCALE2
    slot_pos = lax.broadcasted_iota(jnp.int32, (QROWS, HD), 1)
    block_top, weights = [], []
    for b in range(GROUP):
        alive = slot_pos < live[step * GROUP + b]
        s = jnp.where(alive, scores[b * QROWS : (b + 1) * QROWS], LOW)
        highest = jnp.max(s, axis=-1, keepdims=True)
        block_top.append(jnp.broadcast_to(highest, (QROWS, HD)))
        weights.append(jnp.where(alive, jnp.exp2(s - highest), 0.0))
    result = jnp.dot(
        jnp.concatenate(weights, axis=0).astype(jnp.bfloat16),
        values,
        preferred_element_type=jnp.float32,
    )
    for b in range(GROUP):
        r = reqs[b]
        part = result[b * QROWS : (b + 1) * QROWS, b * HD : (b + 1) * HD]
        part_sum = jnp.sum(weights[b], axis=-1, keepdims=True)
        old_top = top[r]
        new_top = jnp.maximum(old_top, block_top[b])
        old_factor = jnp.exp2(old_top - new_top)
        new_factor = jnp.exp2(block_top[b] - new_top)
        top[r] = new_top
        total[r] = total[r] * old_factor + part_sum * new_factor
        mixed[r] = mixed[r] * old_factor + part * new_factor

    @pl.when(step == pl.num_programs(0) - 1)
    def _():
        sums = total[...]
        held = sums > 0.0
        safe = jnp.where(held, sums, 1.0)
        level = jnp.where(held, top[...] + jnp.log2(safe), LOW)
        first = level.astype(jnp.bfloat16).astype(jnp.float32)
        second = (level - first).astype(jnp.bfloat16).astype(jnp.float32)
        third = level - first - second
        lane = lax.broadcasted_iota(jnp.int32, level.shape, 2)
        terms = jnp.where(lane == 0, first, jnp.where(lane == 1, second, third))
        out_ref[...] = jnp.concatenate([mixed[...] / safe, terms], axis=1).astype(jnp.bfloat16)


def decode_cache(owner, live, queries, k_cache, v_cache):
    req_count, block_count = queries.shape[0], k_cache.shape[0]
    state = pltpu.VMEM((req_count, QROWS, HD), jnp.float32)
    return pl.pallas_call(
        decode_kernel,
        out_shape=jax.ShapeDtypeStruct((req_count, 2 * QROWS, HD), jnp.bfloat16),
        grid_spec=pltpu.PrefetchScalarGridSpec(
            num_scalar_prefetch=2,
            grid=(block_count // GROUP,),
            in_specs=[
                pl.BlockSpec((req_count, QROWS, HD), lambda i, *_: (0, 0, 0)),
                pl.BlockSpec((GROUP, HD, HD), lambda i, *_: (i, 0, 0)),
                pl.BlockSpec((GROUP, HD, HD), lambda i, *_: (i, 0, 0)),
            ],
            out_specs=pl.BlockSpec((req_count, 2 * QROWS, HD), lambda i, *_: (0, 0, 0)),
            scratch_shapes=[pltpu.VMEM((GROUP * QROWS, GROUP * HD), jnp.bfloat16), state, state, state],
        ),
        compiler_params=pltpu.CompilerParams(
            dimension_semantics=("arbitrary",), vmem_limit_bytes=32 << 20
        ),
        cost_estimate=pl.CostEstimate(
            flops=1 << 32, bytes_accessed=9 << 20, transcendentals=1 << 20
        ),
    )(owner, live, queries, k_cache, v_cache)


def merge_kernel(parts_ref, q_ref, k_ref, v_ref, out_ref):
    source_count, req_count = parts_ref.shape[0], parts_ref.shape[1]
    for r in range(req_count):
        queries = q_ref[r]
        row = lax.broadcasted_iota(jnp.int32, (QROWS, 1), 0)
        levels, pieces = [], []
        for s in range(source_count):
            both = parts_ref[s, r].astype(jnp.float32)
            terms = both[QROWS:]
            levels.append(terms[:, 0:1] + terms[:, 1:2] + terms[:, 2:3])
            pieces.append(both[:QROWS])
        for n in range(2):
            key = k_ref[n, r : r + 1, :]
            score = jnp.sum(queries * key, axis=-1, keepdims=True) * SCALE2
            if n:
                score = jnp.where(row >= n * HEADS, score, LOW)
            levels.append(score)
            pieces.append(jnp.broadcast_to(v_ref[n, r : r + 1, :], (QROWS, HD)))
        highest = functools.reduce(jnp.maximum, levels)
        shares = [jnp.exp2(level - highest) for level in levels]
        result = functools.reduce(jnp.add, [w * p for w, p in zip(shares, pieces)])
        out_ref[r] = result / functools.reduce(jnp.add, shares)


def decode_merge(parts, queries, k_new, v_new):
    return pl.pallas_call(
        merge_kernel,
        out_shape=jax.ShapeDtypeStruct(queries.shape, jnp.float32),
        in_specs=[VMEM] * 4,
        out_specs=VMEM,
    )(parts, queries, k_new.astype(jnp.float32), v_new.astype(jnp.float32))


def body(
    q_prefill,
    k_prefill,
    v_prefill,
    q_decode,
    k_new,
    v_new,
    k_cache,
    v_cache,
    block_table,
    req_lengths,
):
    me = lax.axis_index("inst")
    z, y, c = me // 8, (me // 2) % 4, me % 2
    steps, req_local, _ = q_decode.shape

    own_queries = q_decode.reshape(steps, req_local, HEADS, HD).transpose(1, 0, 2, 3)
    own_queries = own_queries.reshape(req_local, QROWS, HD)
    every_query = lax.all_gather(own_queries, "inst", axis=0, tiled=True)

    own = jnp.concatenate([k_prefill, v_prefill], axis=1)
    up = permute(own, moves(0, 1, 0))
    down = permute(own, moves(0, -1, 0))
    across = permute(own, moves(1, 0, 0))
    beside = permute(own, moves(0, 0, 1))
    mirror = [(i, 15 - i) for i in range(16)]
    other_rows = permute(q_prefill[ROWS:], mirror)
    queries = jnp.stack([q_prefill[:ROWS], other_rows])

    up_more = permute(jnp.concatenate([across, up[:ROWS]]), moves(0, 1, 0))
    down_more = permute(jnp.concatenate([across, down[ROWS:]]), moves(0, -1, 0))
    beside_near = permute(jnp.concatenate([up, down, across]), moves(0, 0, 1))

    limits = jnp.stack([me, 15 - me])
    near_ids = [
        me,
        index_of(z, y, c + 1),
        index_of(z, y + 3, c),
        index_of(z, y + 1, c),
        index_of(z + 1, y, c),
        index_of(z, y + 3, c + 1),
        index_of(z, y + 1, c + 1),
        index_of(z + 1, y, c + 1),
    ]
    near_meta = jnp.concatenate([jnp.stack(near_ids), limits, jnp.zeros((1,), jnp.int32)])
    near_sources = [(k, 0, KEYS, k, 0) for k in range(5)]
    near_sources += [(5, k * KEYS, KEYS, 5 + k, 0) for k in range(3)]
    state = flash(
        near_meta.astype(jnp.int32),
        queries,
        [own, beside, up, down, across, beside_near],
        near_sources,
        diag=(0, 0),
    )

    up_last = permute(up_more[:ROWS], moves(0, 1, 0))
    down_last = permute(down_more[ROWS:KEYS], moves(0, -1, 0))
    beside_far = permute(jnp.concatenate([up_more, down_more]), moves(0, 0, 1))
    beside_last = permute(jnp.concatenate([up_last, down_last]), moves(0, 0, 1))
    far_ids = [
        index_of(z, y + 2, c),
        index_of(z + 1, y + 3, c),
        index_of(z + 1, y + 1, c),
        index_of(z + 1, y + 2, c),
        index_of(z, y + 2, c + 1),
        index_of(z + 1, y + 3, c + 1),
        index_of(z + 1, y + 1, c + 1),
        index_of(z + 1, y + 2, c + 1),
    ]
    far_arrays = [up_more, down_more, up_last, down_last, beside_far, beside_last]
    both = KEYS + ROWS
    far_sources = [
        (0, KEYS, ROWS, 0, 0),
        (1, KEYS, ROWS, 0, ROWS),
        (0, 0, KEYS, 1, 0),
        (1, 0, KEYS, 2, 0),
        (2, 0, ROWS, 3, 0),
        (3, 0, ROWS, 3, ROWS),
        (4, KEYS, ROWS, 4, 0),
        (4, both + KEYS, ROWS, 4, ROWS),
        (4, 0, KEYS, 5, 0),
        (4, both, KEYS, 6, 0),
        (5, 0, KEYS, 7, 0),
    ]
    mirror_slot = jnp.where(y % 2 == 0, 5, 6)
    far_ids = jnp.stack(far_ids)
    other_meta = jnp.concatenate([far_ids, limits[1:], mirror_slot[None]]).astype(jnp.int32)
    own_meta = jnp.concatenate([far_ids, limits[:1], mirror_slot[None]]).astype(jnp.int32)
    (other_out,) = flash(
        other_meta,
        queries[1:],
        far_arrays,
        far_sources,
        state=[part[1:] for part in state],
        final=True,
        diag=(0, ROWS),
    )
    last_rows = permute(other_out[0], mirror)
    (own_out,) = flash(
        own_meta,
        queries[:1],
        far_arrays,
        far_sources,
        state=[part[:1] for part in state],
        final=True,
    )

    block_count, block_len = k_cache.shape[:2]
    width = block_table.shape[1]
    global_id = me * block_count + jnp.arange(block_count, dtype=jnp.int32)
    matches = block_table.reshape(-1)[None, :] == global_id[:, None]
    place = jnp.arange(block_table.size, dtype=jnp.int32)[None, :]
    flat = jnp.sum(jnp.where(matches, place, 0), axis=1)
    owner = flat // width
    left = req_lengths[:, None] - jnp.arange(width, dtype=jnp.int32)[None, :] * block_len
    left = jnp.clip(left, 0, block_len).reshape(-1)
    live = jnp.sum(jnp.where(matches, left[None, :], 0), axis=1)
    parts = decode_cache(owner, live, every_query.astype(jnp.float32), k_cache, v_cache)
    parts = lax.all_to_all(parts, "inst", 0, 0, tiled=True)
    parts = parts.reshape(-1, req_local, 2 * QROWS, HD)
    result = decode_merge(parts, own_queries.astype(jnp.float32), k_new, v_new)
    result = result.astype(jnp.bfloat16).reshape(req_local, steps, HEADS * HD)
    decode_out = result.transpose(1, 0, 2)

    prefill_out = jnp.concatenate([own_out[0], last_rows])
    return prefill_out, decode_out


def solution(mesh):
    placed = (
        P("inst", "tp"),
        P("inst", "tp"),
        P("inst", "tp"),
        P(None, "inst", "tp"),
        P(None, "inst", "tp"),
        P(None, "inst", "tp"),
        P("inst", None, "tp"),
        P("inst", None, "tp"),
        P(),
        P(),
    )
    return jax.shard_map(
        body,
        mesh=mesh,
        in_specs=placed,
        out_specs=(P("inst", "tp"), P(None, "inst", "tp")),
        check_vma=False,
    )
```

```python
import functools
import math

import jax
import jax.numpy as jnp
from jax import lax
from jax.experimental import pallas as pl
from jax.experimental.pallas import tpu as pltpu
from jax.sharding import PartitionSpec as P

HD = 128
SCALE2 = HD**-0.5 * math.log2(math.e)
LOW = -1e30
HEADS = 4
ROWS = 512
KEYS = 1024
CHUNK = 256
SLOTS = 8
VMEM = pl.BlockSpec(memory_space=pltpu.VMEM)
SMEM = pl.BlockSpec(memory_space=pltpu.SMEM)
ANY = pl.BlockSpec(memory_space=pl.ANY)
TINY = pl.CostEstimate(flops=1, bytes_accessed=1, transcendentals=0)
NT = (((1,), (1,)), ((), ()))


def index_of(z, y, c):
    return (z % 2) * 8 + (y % 4) * 2 + c % 2


def moves(dz, dy, dc):
    return [
        (index_of(z, y, c), index_of(z + dz, y + dy, c + dc))
        for z in range(2)
        for y in range(4)
        for c in range(2)
    ]


def permute(value, pairs):
    return lax.ppermute(value, "inst", pairs)


def after(values, earlier):
    return lax.optimization_barrier((*values, *earlier))[: len(values)]


def flash_kernel(half_count, sources, has_state, final, diag, diag_slot, *refs):
    refs = list(refs)
    meta = refs.pop(0)
    first_id = SLOTS if has_state else 0
    q_refs = [refs.pop(0) for _ in range(half_count)]
    kv_refs = [refs.pop(0) for _ in range(1 + max(src for src, *_ in sources))]
    state_in = [refs.pop(0) for _ in range(2)] if has_state else None
    outs = [refs.pop(0) for _ in range(half_count if final else 2)]
    kv, qs, acc, top, scores, row_top, items, sem, *old = refs

    copies = [
        pltpu.make_async_copy(
            kv_refs[src].at[pl.ds(first, count)],
            kv.at[slot, pl.ds(row, count)],
            sem.at[k],
        )
        for k, (src, first, count, slot, row) in enumerate(sources)
    ]
    for copy in copies:
        copy.start()
    state_copies = []
    if has_state:
        state_copies = [
            pltpu.make_async_copy(state_in[k], old[k], sem.at[len(sources) + k]) for k in range(2)
        ]
    for copy in state_copies:
        copy.start()

    for half in range(half_count):
        for h in range(HEADS):
            scaled = q_refs[half][:ROWS, h * HD : (h + 1) * HD].astype(jnp.float32) * SCALE2
            high = scaled.astype(jnp.bfloat16)
            qs[half, h, :, :HD] = high
            qs[half, h, :, HD:] = (scaled - high.astype(jnp.float32)).astype(jnp.bfloat16)
    acc[...] = jnp.zeros_like(acc)
    top[...] = jnp.full_like(top, LOW)

    count = jnp.int32(0)
    for half in range(half_count):
        limit = meta[2 * SLOTS + half]
        for slot in range(SLOTS):
            wanted = meta[first_id + slot] < limit

            @pl.when(wanted)
            def _(count=count, half=half, slot=slot):
                items[count] = half * SLOTS + slot

            count = count + wanted.astype(jnp.int32)

    for copy in copies if diag_slot is None else copies[:1]:
        copy.wait()

    ones = jnp.ones((KEYS, HD), jnp.bfloat16)

    def update(half, h, row, s, new_top, values):
        old_top = top[half, h, pl.ds(row, CHUNK), :]
        new_top = jnp.maximum(old_top, new_top)
        factor = jnp.exp2(old_top - new_top)
        weights = jnp.exp2(s - new_top[:, :1])
        top[half, h, pl.ds(row, CHUNK), :] = new_top
        mixed = jnp.dot(
            weights.astype(jnp.bfloat16),
            jnp.concatenate([values, ones[: values.shape[0]]], axis=1),
            preferred_element_type=jnp.float32,
        )
        for part in range(2):
            cols = slice(part * HD, (part + 1) * HD)
            acc[half, h, pl.ds(row, CHUNK), cols] = (
                acc[half, h, pl.ds(row, CHUNK), cols] * factor + mixed[:, cols]
            )

    if diag is not None:
        half, first_row = diag
        slot = meta[2 * SLOTS + half_count] if diag_slot is None else diag_slot
        for r in range(ROWS // CHUNK):
            seen = first_row + (r + 1) * CHUNK
            key_rows = kv[slot, :seen, :HD]
            key_rows = jnp.concatenate([key_rows, key_rows], axis=1)
            row_pos = lax.broadcasted_iota(jnp.int32, (CHUNK, seen), 0) + (seen - CHUNK)
            allowed = lax.broadcasted_iota(jnp.int32, (CHUNK, seen), 1) <= row_pos
            for h in range(HEADS):
                s = lax.dot_general(
                    qs[half, h, r * CHUNK : (r + 1) * CHUNK, :],
                    key_rows,
                    NT,
                    preferred_element_type=jnp.float32,
                )
                s = jnp.where(allowed, s, LOW)
                update(
                    half, h, r * CHUNK, s, jnp.max(s, axis=-1, keepdims=True), kv[slot, :seen, HD:]
                )

    for copy in [] if diag_slot is None else copies[1:]:
        copy.wait()

    def place(item):
        code = items[item]
        return code // SLOTS, code % SLOTS

    def produce(item, r):
        half, slot = place(item)
        key_rows = kv[slot, :, :HD]
        key_rows = jnp.concatenate([key_rows, key_rows], axis=1)
        for h in range(HEADS):
            s = lax.dot_general(
                qs[half, h, r * CHUNK : (r + 1) * CHUNK, :],
                key_rows,
                NT,
                preferred_element_type=jnp.float32,
            )
            scores[r, h] = s
            row_top[r, h] = jnp.broadcast_to(jnp.max(s, axis=-1, keepdims=True), (CHUNK, HD))

    def consume(item, r):
        half, slot = place(item)
        for h in range(HEADS):
            update(half, h, r * CHUNK, scores[r, h], row_top[r, h], kv[slot, :, HD:])

    @pl.when(count > 0)
    def _():
        produce(0, 0)

        @pl.loop(0, count)
        def _(item):
            produce(item, 1)
            consume(item, 0)
            produce(jnp.minimum(item + 1, count - 1), 0)
            consume(item, 1)

    for copy in state_copies:
        copy.wait()
    for half in range(half_count):
        for h in range(HEADS):
            if has_state:
                old_top, old_sum = old[1][half, h, :, :1], old[1][half, h, :, HD - 1 :]
                new_top = jnp.maximum(old_top, top[half, h])
                old_factor = jnp.exp2(old_top - new_top)
                factor = jnp.exp2(top[half, h] - new_top)
                value = acc[half, h, :, :HD] * factor + old[0][half, h] * old_factor
                weight = acc[half, h, :, HD:] * factor + old_sum * old_factor
            else:
                value, weight = acc[half, h, :, :HD], acc[half, h, :, HD:]
            if final:
                outs[half][:ROWS, h * HD : (h + 1) * HD] = (value / weight).astype(jnp.bfloat16)
            else:
                lane = lax.broadcasted_iota(jnp.int32, (ROWS, HD), 1)
                outs[0][half, h] = value
                outs[1][half, h] = jnp.where(lane < HD // 2, top[half, h], weight)


def flash(meta, queries, kv_arrays, sources, state=None, final=False, diag=None, diag_slot=None):
    half_count = len(queries)
    if final:
        out_shape = [
            jax.ShapeDtypeStruct((rows, HEADS * HD), jnp.bfloat16) for rows in (2 * ROWS, ROWS)
        ]
    else:
        out_shape = [jax.ShapeDtypeStruct((half_count, HEADS, ROWS, HD), jnp.float32)] * 2
    operands = [meta, *queries, *kv_arrays, *(state or [])]
    in_specs = [SMEM] + [VMEM] * half_count + [ANY] * (len(kv_arrays) + (2 if state else 0))
    return pl.pallas_call(
        functools.partial(
            flash_kernel, half_count, sources, state is not None, final, diag, diag_slot
        ),
        out_shape=out_shape,
        in_specs=in_specs,
        out_specs=[VMEM] * len(out_shape),
        scratch_shapes=[
            pltpu.VMEM((SLOTS, KEYS, 2 * HD), jnp.bfloat16),
            pltpu.VMEM((half_count, HEADS, ROWS, 2 * HD), jnp.bfloat16),
            pltpu.VMEM((half_count, HEADS, ROWS, 2 * HD), jnp.float32),
            pltpu.VMEM((half_count, HEADS, ROWS, HD), jnp.float32),
            pltpu.VMEM((2, HEADS, CHUNK, KEYS), jnp.float32),
            pltpu.VMEM((2, HEADS, CHUNK, HD), jnp.float32),
            pltpu.SMEM((2 * SLOTS,), jnp.int32),
            pltpu.SemaphoreType.DMA((len(sources) + 2,)),
            *[pltpu.VMEM(part.shape, jnp.float32) for part in state or []],
        ],
        compiler_params=pltpu.CompilerParams(vmem_limit_bytes=58 << 20),
        cost_estimate=TINY,
    )(*operands)


GROUP = 16
QROWS = 8


def decode_kernel(owner, live, q_ref, k_ref, v_ref, out_ref, spread, top, total, mixed):
    step = pl.program_id(0)

    @pl.when(step == 0)
    def _():
        spread[...] = jnp.zeros_like(spread)
        top[...] = jnp.full_like(top, LOW)
        total[...] = jnp.zeros_like(total)
        mixed[...] = jnp.zeros_like(mixed)

    zero = jnp.zeros((QROWS, HD), jnp.float32)
    reqs = [owner[step * GROUP + b] for b in range(GROUP)]
    for b in range(0, GROUP, 2):
        pair = jnp.concatenate(
            [
                jnp.concatenate([q_ref[reqs[b]].astype(jnp.float32), zero], axis=1),
                jnp.concatenate([zero, q_ref[reqs[b + 1]].astype(jnp.float32)], axis=1),
            ],
            axis=0,
        )
        spread[b * QROWS : (b + 2) * QROWS, b * HD : (b + 2) * HD] = pair.astype(jnp.bfloat16)
    keys = jnp.concatenate([k_ref[b] for b in range(GROUP)], axis=1)
    values = jnp.concatenate([v_ref[b] for b in range(GROUP)], axis=1)
    scores = lax.dot_general(spread[...], keys, NT, preferred_element_type=jnp.float32) * SCALE2
    slot_pos = lax.broadcasted_iota(jnp.int32, (QROWS, HD), 1)
    block_top, weights = [], []
    for b in range(GROUP):
        alive = slot_pos < live[step * GROUP + b]
        s = jnp.where(alive, scores[b * QROWS : (b + 1) * QROWS], LOW)
        highest = jnp.max(s, axis=-1, keepdims=True)
        block_top.append(jnp.broadcast_to(highest, (QROWS, HD)))
        weights.append(jnp.where(alive, jnp.exp2(s - highest), 0.0))
    result = jnp.dot(
        jnp.concatenate(weights, axis=0).astype(jnp.bfloat16),
        values,
        preferred_element_type=jnp.float32,
    )
    for b in range(GROUP):
        r = reqs[b]
        part = result[b * QROWS : (b + 1) * QROWS, b * HD : (b + 1) * HD]
        part_sum = jnp.sum(weights[b], axis=-1, keepdims=True)
        old_top = top[r]
        new_top = jnp.maximum(old_top, block_top[b])
        old_factor = jnp.exp2(old_top - new_top)
        new_factor = jnp.exp2(block_top[b] - new_top)
        top[r] = new_top
        total[r] = total[r] * old_factor + part_sum * new_factor
        mixed[r] = mixed[r] * old_factor + part * new_factor

    @pl.when(step == pl.num_programs(0) - 1)
    def _():
        sums = total[...]
        held = sums > 0.0
        safe = jnp.where(held, sums, 1.0)
        level = jnp.where(held, top[...] + jnp.log2(safe), LOW)
        first = level.astype(jnp.bfloat16).astype(jnp.float32)
        second = (level - first).astype(jnp.bfloat16).astype(jnp.float32)
        third = level - first - second
        lane = lax.broadcasted_iota(jnp.int32, level.shape, 2)
        terms = jnp.where(lane == 0, first, jnp.where(lane == 1, second, third))
        out_ref[...] = jnp.concatenate([mixed[...] / safe, terms], axis=1).astype(jnp.bfloat16)


def decode_cache(owner, live, queries, k_cache, v_cache):
    req_count, block_count = queries.shape[0], k_cache.shape[0]
    state = pltpu.VMEM((req_count, QROWS, HD), jnp.float32)
    return pl.pallas_call(
        decode_kernel,
        out_shape=jax.ShapeDtypeStruct((req_count, 2 * QROWS, HD), jnp.bfloat16),
        grid_spec=pltpu.PrefetchScalarGridSpec(
            num_scalar_prefetch=2,
            grid=(block_count // GROUP,),
            in_specs=[
                pl.BlockSpec((req_count, QROWS, HD), lambda i, *_: (0, 0, 0)),
                pl.BlockSpec((GROUP, HD, HD), lambda i, *_: (i, 0, 0)),
                pl.BlockSpec((GROUP, HD, HD), lambda i, *_: (i, 0, 0)),
            ],
            out_specs=pl.BlockSpec((req_count, 2 * QROWS, HD), lambda i, *_: (0, 0, 0)),
            scratch_shapes=[pltpu.VMEM((GROUP * QROWS, GROUP * HD), jnp.bfloat16), state, state, state],
        ),
        compiler_params=pltpu.CompilerParams(
            dimension_semantics=("arbitrary",), vmem_limit_bytes=58 << 20
        ),
        cost_estimate=TINY,
    )(owner, live, queries, k_cache, v_cache)


def merge_kernel(parts_ref, q_ref, k_ref, v_ref, out_ref):
    source_count, req_count = parts_ref.shape[0], parts_ref.shape[1]
    k_new, v_new = k_ref[...].astype(jnp.float32), v_ref[...].astype(jnp.float32)
    for r in range(req_count):
        queries = q_ref[r].astype(jnp.float32)
        row = lax.broadcasted_iota(jnp.int32, (QROWS, 1), 0)
        levels, pieces = [], []
        for s in range(source_count):
            both = parts_ref[s, r].astype(jnp.float32)
            terms = both[QROWS:]
            levels.append(terms[:, 0:1] + terms[:, 1:2] + terms[:, 2:3])
            pieces.append(both[:QROWS])
        for n in range(2):
            key = k_new[n, r : r + 1, :]
            score = jnp.sum(queries * key, axis=-1, keepdims=True) * SCALE2
            if n:
                score = jnp.where(row >= n * HEADS, score, LOW)
            levels.append(score)
            pieces.append(jnp.broadcast_to(v_new[n, r : r + 1, :], (QROWS, HD)))
        highest = functools.reduce(jnp.maximum, levels)
        shares = [jnp.exp2(level - highest) for level in levels]
        result = functools.reduce(jnp.add, [w * p for w, p in zip(shares, pieces)])
        out_ref[r] = (result / functools.reduce(jnp.add, shares)).astype(jnp.bfloat16)


def decode_merge(parts, queries, k_new, v_new):
    return pl.pallas_call(
        merge_kernel,
        out_shape=jax.ShapeDtypeStruct(queries.shape, jnp.bfloat16),
        in_specs=[VMEM] * 4,
        out_specs=VMEM,
        cost_estimate=TINY,
    )(parts, queries, k_new, v_new)


def body(
    q_prefill,
    k_prefill,
    v_prefill,
    q_decode,
    k_new,
    v_new,
    k_cache,
    v_cache,
    block_table,
    req_lengths,
):
    me = lax.axis_index("inst")
    z, y, c = me // 8, (me // 2) % 4, me % 2
    steps, req_local, _ = q_decode.shape

    own_queries = q_decode.reshape(steps, req_local, HEADS, HD).transpose(1, 0, 2, 3)
    own_queries = own_queries.reshape(req_local, QROWS, HD)
    copies = jnp.broadcast_to(own_queries, (16, req_local, QROWS, HD)).reshape(-1, QROWS, HD)
    every_query = lax.all_to_all(copies, "inst", 0, 0, tiled=True)

    own = jnp.concatenate([k_prefill, v_prefill], axis=1)
    up = permute(own, moves(0, 1, 0))
    down = permute(own, moves(0, -1, 0))
    across = permute(own, moves(1, 0, 0))
    beside = permute(own, moves(0, 0, 1))
    up, down, across = after([up, down, across], [every_query])
    mirror = [(i, 15 - i) for i in range(16)]
    up_more = permute(jnp.concatenate([across, up[:ROWS]]), moves(0, 1, 0))
    down_more = permute(jnp.concatenate([across, down[ROWS:]]), moves(0, -1, 0))
    beside_near = permute(jnp.concatenate([up, down, across]), moves(0, 0, 1))
    block_count, block_len = k_cache.shape[:2]
    width = block_table.shape[1]
    global_id = me * block_count + jnp.arange(block_count, dtype=jnp.int32)
    matches = block_table.reshape(-1)[None, :] == global_id[:, None]
    place = jnp.arange(block_table.size, dtype=jnp.int32)[None, :]
    flat = jnp.sum(jnp.where(matches, place, 0), axis=1)
    owner = flat // width
    left = req_lengths[:, None] - jnp.arange(width, dtype=jnp.int32)[None, :] * block_len
    left = jnp.clip(left, 0, block_len).reshape(-1)
    live = jnp.sum(jnp.where(matches, left[None, :], 0), axis=1)
    every_query = after([every_query], [beside_near])[0]
    parts = decode_cache(owner, live, every_query, k_cache, v_cache)
    received = lax.all_to_all(parts, "inst", 0, 0, tiled=True)

    second_rows = after([q_prefill], [parts])[0][ROWS:]
    other_rows = permute(second_rows, mirror)
    queries = [q_prefill, other_rows]

    up_more, down_more = after([up_more, down_more], [second_rows])
    up_last = permute(up_more[:KEYS], moves(0, 1, 0))
    down_last = permute(down_more[:KEYS], moves(0, -1, 1))
    beside_far = permute(jnp.concatenate([up_more, down_more]), moves(0, 0, 1))

    near_ids = [
        me,
        index_of(z, y, c + 1),
        index_of(z, y + 3, c),
        index_of(z, y + 1, c),
        index_of(z + 1, y, c),
        index_of(z, y + 3, c + 1),
        index_of(z, y + 1, c + 1),
        index_of(z + 1, y, c + 1),
    ]
    far_ids = [
        index_of(z, y + 2, c),
        index_of(z + 1, y + 3, c),
        index_of(z + 1, y + 1, c),
        index_of(z + 1, y + 2, c),
        index_of(z, y + 2, c + 1),
        index_of(z + 1, y + 3, c + 1),
        index_of(z + 1, y + 1, c + 1),
        index_of(z + 1, y + 2, c + 1),
    ]
    near_sources = [(k, 0, KEYS, k, 0) for k in range(5)]
    near_sources += [(5, k * KEYS, KEYS, 5 + k, 0) for k in range(3)]
    mirror_slot = jnp.where(y % 2 == 0, 5, 6)
    numbers = jnp.stack([*near_ids, *far_ids, me, 15 - me, mirror_slot]).astype(jnp.int32)
    own = after([own], [parts])[0]
    state = flash(
        numbers,
        queries,
        [own, beside, up, down, across, beside_near],
        near_sources,
        diag=(0, 0),
        diag_slot=0,
    )

    both = KEYS + ROWS
    far_sources = [
        (0, KEYS, ROWS, 0, 0),
        (1, KEYS, ROWS, 0, ROWS),
        (0, 0, KEYS, 1, 0),
        (1, 0, KEYS, 2, 0),
        (2, 0, KEYS, 3, 0),
        (4, KEYS, ROWS, 4, 0),
        (4, both + KEYS, ROWS, 4, ROWS),
        (4, 0, KEYS, 5, 0),
        (4, both, KEYS, 6, 0),
        (3, 0, KEYS, 7, 0),
    ]
    *state, received = lax.optimization_barrier((*state, received))
    received = received.reshape(-1, req_local, 2 * QROWS, HD)
    decode_out = decode_merge(received, own_queries, k_new, v_new)
    decode_out = decode_out.reshape(req_local, steps, HEADS * HD).transpose(1, 0, 2)

    own_out, other_out = flash(
        numbers,
        queries,
        [up_more, down_more, up_last, down_last, beside_far],
        far_sources,
        state=state,
        final=True,
        diag=(1, ROWS),
    )
    last_rows = permute(other_out, mirror)
    return lax.dynamic_update_slice(own_out, last_rows, (ROWS, 0)), decode_out


def solution(mesh):
    placed = (
        P("inst", "tp"),
        P("inst", "tp"),
        P("inst", "tp"),
        P(None, "inst", "tp"),
        P(None, "inst", "tp"),
        P(None, "inst", "tp"),
        P("inst", None, "tp"),
        P("inst", None, "tp"),
        P(),
        P(),
    )
    return jax.shard_map(
        body,
        mesh=mesh,
        in_specs=placed,
        out_specs=(P("inst", "tp"), P(None, "inst", "tp")),
        check_vma=False,
    )
```

```python
import functools
import math

import jax
import jax.numpy as jnp
from jax import lax
from jax.experimental import pallas as pl
from jax.experimental.pallas import tpu as pltpu
from jax.sharding import PartitionSpec as P

HD = 128
SCALE2 = HD**-0.5 * math.log2(math.e)
LOW = -1e30
HEADS = 4
ROWS = 512
KEYS = 1024
CHUNK = 256
SLOTS = 8
VMEM = pl.BlockSpec(memory_space=pltpu.VMEM)
SMEM = pl.BlockSpec(memory_space=pltpu.SMEM)
ANY = pl.BlockSpec(memory_space=pl.ANY)
TINY = pl.CostEstimate(flops=1, bytes_accessed=1, transcendentals=0)
LONG = pl.CostEstimate(flops=1 << 35, bytes_accessed=1 << 24, transcendentals=1 << 24)
NT = (((1,), (1,)), ((), ()))


def index_of(z, y, c):
    return (z % 2) * 8 + (y % 4) * 2 + c % 2


def moves(dz, dy, dc):
    return [
        (index_of(z, y, c), index_of(z + dz, y + dy, c + dc))
        for z in range(2)
        for y in range(4)
        for c in range(2)
    ]


def permute(value, pairs):
    return lax.ppermute(value, "inst", pairs)


def after(values, earlier):
    return lax.optimization_barrier((*values, *earlier))[: len(values)]


def flash_kernel(half_count, sources, has_state, final, diag, diag_slot, *refs):
    refs = list(refs)
    meta = refs.pop(0)
    first_id = SLOTS if has_state else 0
    q_refs = [refs.pop(0) for _ in range(half_count)]
    kv_refs = [refs.pop(0) for _ in range(1 + max(src for src, *_ in sources))]
    state_in = [refs.pop(0) for _ in range(2)] if has_state else None
    outs = [refs.pop(0) for _ in range(half_count if final else 2)]
    kv, qs, acc, top, scores, row_top, items, sem, *old = refs

    copies = [
        pltpu.make_async_copy(
            kv_refs[src].at[pl.ds(first, count)],
            kv.at[slot, pl.ds(row, count)],
            sem.at[k],
        )
        for k, (src, first, count, slot, row) in enumerate(sources)
    ]
    for copy in copies:
        copy.start()
    state_copies = []
    if has_state:
        state_copies = [
            pltpu.make_async_copy(state_in[k], old[k], sem.at[len(sources) + k]) for k in range(2)
        ]
    for copy in state_copies:
        copy.start()

    for half in range(half_count):
        for h in range(HEADS):
            scaled = q_refs[half][:ROWS, h * HD : (h + 1) * HD].astype(jnp.float32) * SCALE2
            high = scaled.astype(jnp.bfloat16)
            qs[half, h, :, :HD] = high
            qs[half, h, :, HD:] = (scaled - high.astype(jnp.float32)).astype(jnp.bfloat16)
    acc[...] = jnp.zeros_like(acc)
    top[...] = jnp.full_like(top, LOW)

    count = jnp.int32(0)
    for half in range(half_count):
        limit = meta[2 * SLOTS + half]
        for slot in range(SLOTS):
            wanted = meta[first_id + slot] < limit

            @pl.when(wanted)
            def _(count=count, half=half, slot=slot):
                items[count] = half * SLOTS + slot

            count = count + wanted.astype(jnp.int32)

    for copy in copies if diag_slot is None else copies[:1]:
        copy.wait()

    ones = jnp.ones((KEYS, HD), jnp.bfloat16)

    def update(half, h, row, s, new_top, values):
        old_top = top[half, h, pl.ds(row, CHUNK), :]
        new_top = jnp.maximum(old_top, new_top)
        factor = jnp.exp2(old_top - new_top)
        weights = jnp.exp2(s - new_top[:, :1])
        top[half, h, pl.ds(row, CHUNK), :] = new_top
        mixed = jnp.dot(
            weights.astype(jnp.bfloat16),
            jnp.concatenate([values, ones[: values.shape[0]]], axis=1),
            preferred_element_type=jnp.float32,
        )
        for part in range(2):
            cols = slice(part * HD, (part + 1) * HD)
            acc[half, h, pl.ds(row, CHUNK), cols] = (
                acc[half, h, pl.ds(row, CHUNK), cols] * factor + mixed[:, cols]
            )

    if diag is not None:
        half, first_row = diag
        slot = meta[2 * SLOTS + half_count] if diag_slot is None else diag_slot
        for r in range(ROWS // CHUNK):
            seen = first_row + (r + 1) * CHUNK
            key_rows = kv[slot, :seen, :HD]
            key_rows = jnp.concatenate([key_rows, key_rows], axis=1)
            row_pos = lax.broadcasted_iota(jnp.int32, (CHUNK, seen), 0) + (seen - CHUNK)
            allowed = lax.broadcasted_iota(jnp.int32, (CHUNK, seen), 1) <= row_pos
            for h in range(HEADS):
                s = lax.dot_general(
                    qs[half, h, r * CHUNK : (r + 1) * CHUNK, :],
                    key_rows,
                    NT,
                    preferred_element_type=jnp.float32,
                )
                s = jnp.where(allowed, s, LOW)
                update(
                    half, h, r * CHUNK, s, jnp.max(s, axis=-1, keepdims=True), kv[slot, :seen, HD:]
                )

    for copy in [] if diag_slot is None else copies[1:]:
        copy.wait()

    def place(item):
        code = items[item]
        return code // SLOTS, code % SLOTS

    def produce(item, r):
        half, slot = place(item)
        key_rows = kv[slot, :, :HD]
        key_rows = jnp.concatenate([key_rows, key_rows], axis=1)
        for h in range(HEADS):
            s = lax.dot_general(
                qs[half, h, r * CHUNK : (r + 1) * CHUNK, :],
                key_rows,
                NT,
                preferred_element_type=jnp.float32,
            )
            scores[r, h] = s
            row_top[r, h] = jnp.broadcast_to(jnp.max(s, axis=-1, keepdims=True), (CHUNK, HD))

    def consume(item, r):
        half, slot = place(item)
        for h in range(HEADS):
            update(half, h, r * CHUNK, scores[r, h], row_top[r, h], kv[slot, :, HD:])

    @pl.when(count > 0)
    def _():
        produce(0, 0)

        @pl.loop(0, count)
        def _(item):
            produce(item, 1)
            consume(item, 0)
            produce(jnp.minimum(item + 1, count - 1), 0)
            consume(item, 1)

    for copy in state_copies:
        copy.wait()
    for half in range(half_count):
        for h in range(HEADS):
            if has_state:
                old_top, old_sum = old[1][half, h, :, :1], old[1][half, h, :, HD - 1 :]
                new_top = jnp.maximum(old_top, top[half, h])
                old_factor = jnp.exp2(old_top - new_top)
                factor = jnp.exp2(top[half, h] - new_top)
                value = acc[half, h, :, :HD] * factor + old[0][half, h] * old_factor
                weight = acc[half, h, :, HD:] * factor + old_sum * old_factor
            else:
                value, weight = acc[half, h, :, :HD], acc[half, h, :, HD:]
            if final:
                outs[half][:ROWS, h * HD : (h + 1) * HD] = (value / weight).astype(jnp.bfloat16)
            else:
                lane = lax.broadcasted_iota(jnp.int32, (ROWS, HD), 1)
                outs[0][half, h] = value
                outs[1][half, h] = jnp.where(lane < HD // 2, top[half, h], weight)


def flash(meta, queries, kv_arrays, sources, state=None, final=False, diag=None, diag_slot=None):
    half_count = len(queries)
    if final:
        out_shape = [
            jax.ShapeDtypeStruct((rows, HEADS * HD), jnp.bfloat16) for rows in (2 * ROWS, ROWS)
        ]
    else:
        out_shape = [jax.ShapeDtypeStruct((half_count, HEADS, ROWS, HD), jnp.float32)] * 2
    operands = [meta, *queries, *kv_arrays, *(state or [])]
    in_specs = [SMEM] + [VMEM] * half_count + [ANY] * (len(kv_arrays) + (2 if state else 0))
    return pl.pallas_call(
        functools.partial(
            flash_kernel, half_count, sources, state is not None, final, diag, diag_slot
        ),
        out_shape=out_shape,
        in_specs=in_specs,
        out_specs=[VMEM] * len(out_shape),
        scratch_shapes=[
            pltpu.VMEM((SLOTS, KEYS, 2 * HD), jnp.bfloat16),
            pltpu.VMEM((half_count, HEADS, ROWS, 2 * HD), jnp.bfloat16),
            pltpu.VMEM((half_count, HEADS, ROWS, 2 * HD), jnp.float32),
            pltpu.VMEM((half_count, HEADS, ROWS, HD), jnp.float32),
            pltpu.VMEM((2, HEADS, CHUNK, KEYS), jnp.float32),
            pltpu.VMEM((2, HEADS, CHUNK, HD), jnp.float32),
            pltpu.SMEM((2 * SLOTS,), jnp.int32),
            pltpu.SemaphoreType.DMA((len(sources) + 2,)),
            *[pltpu.VMEM(part.shape, jnp.float32) for part in state or []],
        ],
        compiler_params=pltpu.CompilerParams(vmem_limit_bytes=58 << 20),
        cost_estimate=TINY if final else LONG,
    )(*operands)


GROUP = 16
QROWS = 8


def decode_kernel(owner, live, q_ref, k_ref, v_ref, out_ref, spread, top, total, mixed):
    step = pl.program_id(0)

    @pl.when(step == 0)
    def _():
        spread[...] = jnp.zeros_like(spread)
        top[...] = jnp.full_like(top, LOW)
        total[...] = jnp.zeros_like(total)
        mixed[...] = jnp.zeros_like(mixed)

    zero = jnp.zeros((QROWS, HD), jnp.float32)
    reqs = [owner[step * GROUP + b] for b in range(GROUP)]
    for b in range(0, GROUP, 2):
        pair = jnp.concatenate(
            [
                jnp.concatenate([q_ref[reqs[b]].astype(jnp.float32), zero], axis=1),
                jnp.concatenate([zero, q_ref[reqs[b + 1]].astype(jnp.float32)], axis=1),
            ],
            axis=0,
        )
        spread[b * QROWS : (b + 2) * QROWS, b * HD : (b + 2) * HD] = pair.astype(jnp.bfloat16)
    keys = jnp.concatenate([k_ref[b] for b in range(GROUP)], axis=1)
    values = jnp.concatenate([v_ref[b] for b in range(GROUP)], axis=1)
    scores = lax.dot_general(spread[...], keys, NT, preferred_element_type=jnp.float32) * SCALE2
    slot_pos = lax.broadcasted_iota(jnp.int32, (QROWS, HD), 1)
    block_top, weights = [], []
    for b in range(GROUP):
        alive = slot_pos < live[step * GROUP + b]
        s = jnp.where(alive, scores[b * QROWS : (b + 1) * QROWS], LOW)
        highest = jnp.max(s, axis=-1, keepdims=True)
        block_top.append(jnp.broadcast_to(highest, (QROWS, HD)))
        weights.append(jnp.where(alive, jnp.exp2(s - highest), 0.0))
    result = jnp.dot(
        jnp.concatenate(weights, axis=0).astype(jnp.bfloat16),
        values,
        preferred_element_type=jnp.float32,
    )
    for b in range(GROUP):
        r = reqs[b]
        part = result[b * QROWS : (b + 1) * QROWS, b * HD : (b + 1) * HD]
        part_sum = jnp.sum(weights[b], axis=-1, keepdims=True)
        old_top = top[r]
        new_top = jnp.maximum(old_top, block_top[b])
        old_factor = jnp.exp2(old_top - new_top)
        new_factor = jnp.exp2(block_top[b] - new_top)
        top[r] = new_top
        total[r] = total[r] * old_factor + part_sum * new_factor
        mixed[r] = mixed[r] * old_factor + part * new_factor

    @pl.when(step == pl.num_programs(0) - 1)
    def _():
        sums = total[...]
        held = sums > 0.0
        safe = jnp.where(held, sums, 1.0)
        level = jnp.where(held, top[...] + jnp.log2(safe), LOW)
        first = level.astype(jnp.bfloat16).astype(jnp.float32)
        second = (level - first).astype(jnp.bfloat16).astype(jnp.float32)
        third = level - first - second
        lane = lax.broadcasted_iota(jnp.int32, level.shape, 2)
        terms = jnp.where(lane == 0, first, jnp.where(lane == 1, second, third))
        out_ref[...] = jnp.concatenate([mixed[...] / safe, terms], axis=1).astype(jnp.bfloat16)


def decode_cache(owner, live, queries, k_cache, v_cache):
    req_count, block_count = queries.shape[0], k_cache.shape[0]
    state = pltpu.VMEM((req_count, QROWS, HD), jnp.float32)
    return pl.pallas_call(
        decode_kernel,
        out_shape=jax.ShapeDtypeStruct((req_count, 2 * QROWS, HD), jnp.bfloat16),
        grid_spec=pltpu.PrefetchScalarGridSpec(
            num_scalar_prefetch=2,
            grid=(block_count // GROUP,),
            in_specs=[
                pl.BlockSpec((req_count, QROWS, HD), lambda i, *_: (0, 0, 0)),
                pl.BlockSpec((GROUP, HD, HD), lambda i, *_: (i, 0, 0)),
                pl.BlockSpec((GROUP, HD, HD), lambda i, *_: (i, 0, 0)),
            ],
            out_specs=pl.BlockSpec((req_count, 2 * QROWS, HD), lambda i, *_: (0, 0, 0)),
            scratch_shapes=[pltpu.VMEM((GROUP * QROWS, GROUP * HD), jnp.bfloat16), state, state, state],
        ),
        compiler_params=pltpu.CompilerParams(
            dimension_semantics=("arbitrary",), vmem_limit_bytes=58 << 20
        ),
        cost_estimate=TINY,
    )(owner, live, queries, k_cache, v_cache)


def merge_kernel(parts_ref, q_ref, k_ref, v_ref, out_ref):
    source_count, req_count = parts_ref.shape[0], parts_ref.shape[1]
    k_new, v_new = k_ref[...].astype(jnp.float32), v_ref[...].astype(jnp.float32)
    for r in range(req_count):
        queries = q_ref[r].astype(jnp.float32)
        row = lax.broadcasted_iota(jnp.int32, (QROWS, 1), 0)
        levels, pieces = [], []
        for s in range(source_count):
            both = parts_ref[s, r].astype(jnp.float32)
            terms = both[QROWS:]
            levels.append(terms[:, 0:1] + terms[:, 1:2] + terms[:, 2:3])
            pieces.append(both[:QROWS])
        for n in range(2):
            key = k_new[n, r : r + 1, :]
            score = jnp.sum(queries * key, axis=-1, keepdims=True) * SCALE2
            if n:
                score = jnp.where(row >= n * HEADS, score, LOW)
            levels.append(score)
            pieces.append(jnp.broadcast_to(v_new[n, r : r + 1, :], (QROWS, HD)))
        highest = functools.reduce(jnp.maximum, levels)
        shares = [jnp.exp2(level - highest) for level in levels]
        result = functools.reduce(jnp.add, [w * p for w, p in zip(shares, pieces)])
        out_ref[r] = (result / functools.reduce(jnp.add, shares)).astype(jnp.bfloat16)


def decode_merge(parts, queries, k_new, v_new):
    return pl.pallas_call(
        merge_kernel,
        out_shape=jax.ShapeDtypeStruct(queries.shape, jnp.bfloat16),
        in_specs=[VMEM] * 4,
        out_specs=VMEM,
        cost_estimate=TINY,
    )(parts, queries, k_new, v_new)


def body(
    q_prefill,
    k_prefill,
    v_prefill,
    q_decode,
    k_new,
    v_new,
    k_cache,
    v_cache,
    block_table,
    req_lengths,
):
    me = lax.axis_index("inst")
    z, y, c = me // 8, (me // 2) % 4, me % 2
    steps, req_local, _ = q_decode.shape

    own_queries = q_decode.reshape(steps, req_local, HEADS, HD).transpose(1, 0, 2, 3)
    own_queries = own_queries.reshape(req_local, QROWS, HD)
    copies = jnp.broadcast_to(own_queries, (16, req_local, QROWS, HD)).reshape(-1, QROWS, HD)
    every_query = lax.all_to_all(copies, "inst", 0, 0, tiled=True)

    own = jnp.concatenate([k_prefill, v_prefill], axis=1)
    up = permute(own, moves(0, 1, 0))
    down = permute(own, moves(0, -1, 0))
    across = permute(own, moves(1, 0, 0))
    beside = permute(own, moves(0, 0, 1))
    up, down, across = after([up, down, across], [every_query])
    mirror = [(i, 15 - i) for i in range(16)]
    up_more = permute(jnp.concatenate([across, up[:ROWS]]), moves(0, 1, 0))
    down_more = permute(jnp.concatenate([across, down[ROWS:]]), moves(0, -1, 0))
    beside_near = permute(jnp.concatenate([up, down, across]), moves(0, 0, 1))
    block_count, block_len = k_cache.shape[:2]
    width = block_table.shape[1]
    global_id = me * block_count + jnp.arange(block_count, dtype=jnp.int32)
    matches = block_table.reshape(-1)[None, :] == global_id[:, None]
    place = jnp.arange(block_table.size, dtype=jnp.int32)[None, :]
    flat = jnp.sum(jnp.where(matches, place, 0), axis=1)
    owner = flat // width
    left = req_lengths[:, None] - jnp.arange(width, dtype=jnp.int32)[None, :] * block_len
    left = jnp.clip(left, 0, block_len).reshape(-1)
    live = jnp.sum(jnp.where(matches, left[None, :], 0), axis=1)
    every_query = after([every_query], [beside_near])[0]
    parts = decode_cache(owner, live, every_query, k_cache, v_cache)
    received = lax.all_to_all(parts, "inst", 0, 0, tiled=True)

    second_rows = after([q_prefill], [parts])[0][ROWS:]
    other_rows = permute(second_rows, mirror)
    queries = [q_prefill, other_rows]

    up_more, down_more = after([up_more, down_more], [second_rows])
    up_last = permute(up_more[:KEYS], moves(0, 1, 0))
    down_last = permute(down_more[:KEYS], moves(0, -1, 1))
    beside_far = permute(jnp.concatenate([up_more, down_more]), moves(0, 0, 1))

    near_ids = [
        me,
        index_of(z, y, c + 1),
        index_of(z, y + 3, c),
        index_of(z, y + 1, c),
        index_of(z + 1, y, c),
        index_of(z, y + 3, c + 1),
        index_of(z, y + 1, c + 1),
        index_of(z + 1, y, c + 1),
    ]
    far_ids = [
        index_of(z, y + 2, c),
        index_of(z + 1, y + 3, c),
        index_of(z + 1, y + 1, c),
        index_of(z + 1, y + 2, c),
        index_of(z, y + 2, c + 1),
        index_of(z + 1, y + 3, c + 1),
        index_of(z + 1, y + 1, c + 1),
        index_of(z + 1, y + 2, c + 1),
    ]
    near_sources = [(k, 0, KEYS, k, 0) for k in range(5)]
    near_sources += [(5, k * KEYS, KEYS, 5 + k, 0) for k in range(3)]
    mirror_slot = jnp.where(y % 2 == 0, 5, 6)
    numbers = jnp.stack([*near_ids, *far_ids, me, 15 - me, mirror_slot]).astype(jnp.int32)
    numbers = after([numbers], [parts])[0]
    state = flash(
        numbers,
        queries,
        [own, beside, up, down, across, beside_near],
        near_sources,
        diag=(0, 0),
        diag_slot=0,
    )

    both = KEYS + ROWS
    far_sources = [
        (0, KEYS, ROWS, 0, 0),
        (1, KEYS, ROWS, 0, ROWS),
        (0, 0, KEYS, 1, 0),
        (1, 0, KEYS, 2, 0),
        (2, 0, KEYS, 3, 0),
        (4, KEYS, ROWS, 4, 0),
        (4, both + KEYS, ROWS, 4, ROWS),
        (4, 0, KEYS, 5, 0),
        (4, both, KEYS, 6, 0),
        (3, 0, KEYS, 7, 0),
    ]
    *state, received = lax.optimization_barrier((*state, received))
    received = received.reshape(-1, req_local, 2 * QROWS, HD)
    decode_out = decode_merge(received, own_queries, k_new, v_new)
    decode_out = decode_out.reshape(req_local, steps, HEADS * HD).transpose(1, 0, 2)

    own_out, other_out = flash(
        numbers,
        queries,
        [up_more, down_more, up_last, down_last, beside_far],
        far_sources,
        state=state,
        final=True,
        diag=(1, ROWS),
    )
    last_rows = permute(other_out, mirror)
    return lax.dynamic_update_slice(own_out, last_rows, (ROWS, 0)), decode_out


def solution(mesh):
    placed = (
        P("inst", "tp"),
        P("inst", "tp"),
        P("inst", "tp"),
        P(None, "inst", "tp"),
        P(None, "inst", "tp"),
        P(None, "inst", "tp"),
        P("inst", None, "tp"),
        P("inst", None, "tp"),
        P(),
        P(),
    )
    return jax.shard_map(
        body,
        mesh=mesh,
        in_specs=placed,
        out_specs=(P("inst", "tp"), P(None, "inst", "tp")),
        check_vma=False,
    )
```

```python
import functools
import math

import jax
import jax.numpy as jnp
from jax import lax
from jax.experimental import pallas as pl
from jax.experimental.pallas import tpu as pltpu
from jax.sharding import PartitionSpec as P

HD = 128
SCALE2 = HD**-0.5 * math.log2(math.e)
LOW = -1e30
HEADS = 4
ROWS = 512
KEYS = 1024
CHUNK = 256
SLOTS = 8
VMEM = pl.BlockSpec(memory_space=pltpu.VMEM)
SMEM = pl.BlockSpec(memory_space=pltpu.SMEM)
ANY = pl.BlockSpec(memory_space=pl.ANY)
TINY = pl.CostEstimate(flops=1, bytes_accessed=1, transcendentals=0)
LONG = pl.CostEstimate(flops=1 << 35, bytes_accessed=1 << 24, transcendentals=1 << 24)
NT = (((1,), (1,)), ((), ()))


def index_of(z, y, c):
    return (z % 2) * 8 + (y % 4) * 2 + c % 2


def moves(dz, dy, dc):
    return [
        (index_of(z, y, c), index_of(z + dz, y + dy, c + dc))
        for z in range(2)
        for y in range(4)
        for c in range(2)
    ]


def permute(value, pairs):
    return lax.ppermute(value, "inst", pairs)


def after(values, earlier):
    return lax.optimization_barrier((*values, *earlier))[: len(values)]


def flash_kernel(half_count, sources, has_state, final, diag, diag_slot, *refs):
    refs = list(refs)
    meta = refs.pop(0)
    first_id = SLOTS if has_state else 0
    q_refs = [refs.pop(0) for _ in range(half_count)]
    kv_refs = [refs.pop(0) for _ in range(1 + max(src for src, *_ in sources))]
    state_in = [refs.pop(0) for _ in range(2)] if has_state else None
    outs = [refs.pop(0) for _ in range(half_count if final else 2)]
    kv, qs, acc, top, scores, row_top, items, sem, *old = refs

    copies = [
        pltpu.make_async_copy(
            kv_refs[src].at[pl.ds(first, count)],
            kv.at[slot, pl.ds(row, count)],
            sem.at[k],
        )
        for k, (src, first, count, slot, row) in enumerate(sources)
    ]
    for copy in copies:
        copy.start()
    state_copies = []
    if has_state:
        state_copies = [
            pltpu.make_async_copy(state_in[k], old[k], sem.at[len(sources) + k]) for k in range(2)
        ]
    for copy in state_copies:
        copy.start()

    for half in range(half_count):
        for h in range(HEADS):
            scaled = q_refs[half][:ROWS, h * HD : (h + 1) * HD].astype(jnp.float32) * SCALE2
            high = scaled.astype(jnp.bfloat16)
            qs[half, h, :, :HD] = high
            qs[half, h, :, HD:] = (scaled - high.astype(jnp.float32)).astype(jnp.bfloat16)
    acc[...] = jnp.zeros_like(acc)
    top[...] = jnp.full_like(top, LOW)

    count = jnp.int32(0)
    for half in range(half_count):
        limit = meta[2 * SLOTS + half]
        for slot in range(SLOTS):
            wanted = meta[first_id + slot] < limit

            @pl.when(wanted)
            def _(count=count, half=half, slot=slot):
                items[count] = half * SLOTS + slot

            count = count + wanted.astype(jnp.int32)

    for copy in copies if diag_slot is None else copies[:1]:
        copy.wait()

    ones = jnp.ones((KEYS, HD), jnp.bfloat16)

    def update(half, h, row, s, new_top, values):
        old_top = top[half, h, pl.ds(row, CHUNK), :]
        new_top = jnp.maximum(old_top, new_top)
        factor = jnp.exp2(old_top - new_top)
        weights = jnp.exp2(s - new_top[:, :1])
        top[half, h, pl.ds(row, CHUNK), :] = new_top
        mixed = jnp.dot(
            weights.astype(jnp.bfloat16),
            jnp.concatenate([values, ones[: values.shape[0]]], axis=1),
            preferred_element_type=jnp.float32,
        )
        for part in range(2):
            cols = slice(part * HD, (part + 1) * HD)
            acc[half, h, pl.ds(row, CHUNK), cols] = (
                acc[half, h, pl.ds(row, CHUNK), cols] * factor + mixed[:, cols]
            )

    if diag is not None:
        half, first_row = diag
        slot = meta[2 * SLOTS + half_count] if diag_slot is None else diag_slot
        for r in range(ROWS // CHUNK):
            seen = first_row + (r + 1) * CHUNK
            key_rows = kv[slot, :seen, :HD]
            key_rows = jnp.concatenate([key_rows, key_rows], axis=1)
            row_pos = lax.broadcasted_iota(jnp.int32, (CHUNK, seen), 0) + (seen - CHUNK)
            allowed = lax.broadcasted_iota(jnp.int32, (CHUNK, seen), 1) <= row_pos
            for h in range(HEADS):
                s = lax.dot_general(
                    qs[half, h, r * CHUNK : (r + 1) * CHUNK, :],
                    key_rows,
                    NT,
                    preferred_element_type=jnp.float32,
                )
                s = jnp.where(allowed, s, LOW)
                update(
                    half, h, r * CHUNK, s, jnp.max(s, axis=-1, keepdims=True), kv[slot, :seen, HD:]
                )

    for copy in [] if diag_slot is None else copies[1:]:
        copy.wait()

    def place(item):
        code = items[item]
        return code // SLOTS, code % SLOTS

    def produce(item, r):
        half, slot = place(item)
        key_rows = kv[slot, :, :HD]
        key_rows = jnp.concatenate([key_rows, key_rows], axis=1)
        for h in range(HEADS):
            s = lax.dot_general(
                qs[half, h, r * CHUNK : (r + 1) * CHUNK, :],
                key_rows,
                NT,
                preferred_element_type=jnp.float32,
            )
            scores[r, h] = s
            row_top[r, h] = jnp.broadcast_to(jnp.max(s, axis=-1, keepdims=True), (CHUNK, HD))

    def consume(item, r):
        half, slot = place(item)
        for h in range(HEADS):
            update(half, h, r * CHUNK, scores[r, h], row_top[r, h], kv[slot, :, HD:])

    @pl.when(count > 0)
    def _():
        produce(0, 0)

        @pl.loop(0, count)
        def _(item):
            produce(item, 1)
            consume(item, 0)
            produce(jnp.minimum(item + 1, count - 1), 0)
            consume(item, 1)

    for copy in state_copies:
        copy.wait()
    for half in range(half_count):
        for h in range(HEADS):
            if has_state:
                old_top, old_sum = old[1][half, h, :, :1], old[1][half, h, :, HD - 1 :]
                new_top = jnp.maximum(old_top, top[half, h])
                old_factor = jnp.exp2(old_top - new_top)
                factor = jnp.exp2(top[half, h] - new_top)
                value = acc[half, h, :, :HD] * factor + old[0][half, h] * old_factor
                weight = acc[half, h, :, HD:] * factor + old_sum * old_factor
            else:
                value, weight = acc[half, h, :, :HD], acc[half, h, :, HD:]
            if final:
                outs[half][:ROWS, h * HD : (h + 1) * HD] = (value / weight).astype(jnp.bfloat16)
            else:
                lane = lax.broadcasted_iota(jnp.int32, (ROWS, HD), 1)
                outs[0][half, h] = value
                outs[1][half, h] = jnp.where(lane < HD // 2, top[half, h], weight)


def flash(meta, queries, kv_arrays, sources, state=None, final=False, diag=None, diag_slot=None):
    half_count = len(queries)
    if final:
        out_shape = [
            jax.ShapeDtypeStruct((rows, HEADS * HD), jnp.bfloat16) for rows in (2 * ROWS, ROWS)
        ]
    else:
        out_shape = [jax.ShapeDtypeStruct((half_count, HEADS, ROWS, HD), jnp.float32)] * 2
    operands = [meta, *queries, *kv_arrays, *(state or [])]
    in_specs = [SMEM] + [VMEM] * half_count + [ANY] * (len(kv_arrays) + (2 if state else 0))
    return pl.pallas_call(
        functools.partial(
            flash_kernel, half_count, sources, state is not None, final, diag, diag_slot
        ),
        out_shape=out_shape,
        in_specs=in_specs,
        out_specs=[VMEM] * len(out_shape),
        scratch_shapes=[
            pltpu.VMEM((SLOTS, KEYS, 2 * HD), jnp.bfloat16),
            pltpu.VMEM((half_count, HEADS, ROWS, 2 * HD), jnp.bfloat16),
            pltpu.VMEM((half_count, HEADS, ROWS, 2 * HD), jnp.float32),
            pltpu.VMEM((half_count, HEADS, ROWS, HD), jnp.float32),
            pltpu.VMEM((2, HEADS, CHUNK, KEYS), jnp.float32),
            pltpu.VMEM((2, HEADS, CHUNK, HD), jnp.float32),
            pltpu.SMEM((2 * SLOTS,), jnp.int32),
            pltpu.SemaphoreType.DMA((len(sources) + 2,)),
            *[pltpu.VMEM(part.shape, jnp.float32) for part in state or []],
        ],
        compiler_params=pltpu.CompilerParams(vmem_limit_bytes=58 << 20),
        cost_estimate=TINY if final else LONG,
    )(*operands)


GROUP = 16
QROWS = 8


def decode_kernel(owner, live, q_ref, k_ref, v_ref, out_ref, spread, top, total, mixed):
    step = pl.program_id(0)

    @pl.when(step == 0)
    def _():
        spread[...] = jnp.zeros_like(spread)
        top[...] = jnp.full_like(top, LOW)
        total[...] = jnp.zeros_like(total)
        mixed[...] = jnp.zeros_like(mixed)

    zero = jnp.zeros((QROWS, HD), jnp.float32)
    reqs = [owner[step * GROUP + b] for b in range(GROUP)]
    for b in range(0, GROUP, 2):
        pair = jnp.concatenate(
            [
                jnp.concatenate([q_ref[reqs[b]].astype(jnp.float32), zero], axis=1),
                jnp.concatenate([zero, q_ref[reqs[b + 1]].astype(jnp.float32)], axis=1),
            ],
            axis=0,
        )
        spread[b * QROWS : (b + 2) * QROWS, b * HD : (b + 2) * HD] = pair.astype(jnp.bfloat16)
    keys = jnp.concatenate([k_ref[b] for b in range(GROUP)], axis=1)
    values = jnp.concatenate([v_ref[b] for b in range(GROUP)], axis=1)
    scores = lax.dot_general(spread[...], keys, NT, preferred_element_type=jnp.float32) * SCALE2
    slot_pos = lax.broadcasted_iota(jnp.int32, (QROWS, HD), 1)
    block_top, weights = [], []
    for b in range(GROUP):
        alive = slot_pos < live[step * GROUP + b]
        s = jnp.where(alive, scores[b * QROWS : (b + 1) * QROWS], LOW)
        highest = jnp.max(s, axis=-1, keepdims=True)
        block_top.append(jnp.broadcast_to(highest, (QROWS, HD)))
        weights.append(jnp.where(alive, jnp.exp2(s - highest), 0.0))
    result = jnp.dot(
        jnp.concatenate(weights, axis=0).astype(jnp.bfloat16),
        values,
        preferred_element_type=jnp.float32,
    )
    for b in range(GROUP):
        r = reqs[b]
        part = result[b * QROWS : (b + 1) * QROWS, b * HD : (b + 1) * HD]
        part_sum = jnp.sum(weights[b], axis=-1, keepdims=True)
        old_top = top[r]
        new_top = jnp.maximum(old_top, block_top[b])
        old_factor = jnp.exp2(old_top - new_top)
        new_factor = jnp.exp2(block_top[b] - new_top)
        top[r] = new_top
        total[r] = total[r] * old_factor + part_sum * new_factor
        mixed[r] = mixed[r] * old_factor + part * new_factor

    @pl.when(step == pl.num_programs(0) - 1)
    def _():
        sums = total[...]
        held = sums > 0.0
        safe = jnp.where(held, sums, 1.0)
        level = jnp.where(held, top[...] + jnp.log2(safe), LOW)
        first = level.astype(jnp.bfloat16).astype(jnp.float32)
        second = (level - first).astype(jnp.bfloat16).astype(jnp.float32)
        third = level - first - second
        lane = lax.broadcasted_iota(jnp.int32, level.shape, 2)
        terms = jnp.where(lane == 0, first, jnp.where(lane == 1, second, third))
        out_ref[...] = jnp.concatenate([mixed[...] / safe, terms], axis=1).astype(jnp.bfloat16)


def decode_cache(owner, live, queries, k_cache, v_cache):
    req_count, block_count = queries.shape[0], k_cache.shape[0]
    state = pltpu.VMEM((req_count, QROWS, HD), jnp.float32)
    return pl.pallas_call(
        decode_kernel,
        out_shape=jax.ShapeDtypeStruct((req_count, 2 * QROWS, HD), jnp.bfloat16),
        grid_spec=pltpu.PrefetchScalarGridSpec(
            num_scalar_prefetch=2,
            grid=(block_count // GROUP,),
            in_specs=[
                pl.BlockSpec((req_count, QROWS, HD), lambda i, *_: (0, 0, 0)),
                pl.BlockSpec((GROUP, HD, HD), lambda i, *_: (i, 0, 0)),
                pl.BlockSpec((GROUP, HD, HD), lambda i, *_: (i, 0, 0)),
            ],
            out_specs=pl.BlockSpec((req_count, 2 * QROWS, HD), lambda i, *_: (0, 0, 0)),
            scratch_shapes=[pltpu.VMEM((GROUP * QROWS, GROUP * HD), jnp.bfloat16), state, state, state],
        ),
        compiler_params=pltpu.CompilerParams(
            dimension_semantics=("arbitrary",), vmem_limit_bytes=58 << 20
        ),
        cost_estimate=TINY,
    )(owner, live, queries, k_cache, v_cache)


def merge_kernel(parts_ref, q_ref, k_ref, v_ref, out_ref):
    source_count, req_count = parts_ref.shape[0], parts_ref.shape[1]
    k_new, v_new = k_ref[...].astype(jnp.float32), v_ref[...].astype(jnp.float32)
    for r in range(req_count):
        queries = q_ref[r].astype(jnp.float32)
        row = lax.broadcasted_iota(jnp.int32, (QROWS, 1), 0)
        levels, pieces = [], []
        for s in range(source_count):
            both = parts_ref[s, r].astype(jnp.float32)
            terms = both[QROWS:]
            levels.append(terms[:, 0:1] + terms[:, 1:2] + terms[:, 2:3])
            pieces.append(both[:QROWS])
        for n in range(2):
            key = k_new[n, r : r + 1, :]
            score = jnp.sum(queries * key, axis=-1, keepdims=True) * SCALE2
            if n:
                score = jnp.where(row >= n * HEADS, score, LOW)
            levels.append(score)
            pieces.append(jnp.broadcast_to(v_new[n, r : r + 1, :], (QROWS, HD)))
        highest = functools.reduce(jnp.maximum, levels)
        shares = [jnp.exp2(level - highest) for level in levels]
        result = functools.reduce(jnp.add, [w * p for w, p in zip(shares, pieces)])
        out_ref[r] = (result / functools.reduce(jnp.add, shares)).astype(jnp.bfloat16)


def decode_merge(parts, queries, k_new, v_new):
    return pl.pallas_call(
        merge_kernel,
        out_shape=jax.ShapeDtypeStruct(queries.shape, jnp.bfloat16),
        in_specs=[VMEM] * 4,
        out_specs=VMEM,
        cost_estimate=TINY,
    )(parts, queries, k_new, v_new)


def body(
    q_prefill,
    k_prefill,
    v_prefill,
    q_decode,
    k_new,
    v_new,
    k_cache,
    v_cache,
    block_table,
    req_lengths,
):
    me = lax.axis_index("inst")
    z, y, c = me // 8, (me // 2) % 4, me % 2
    steps, req_local, _ = q_decode.shape

    own_queries = q_decode.reshape(steps, req_local, HEADS, HD).transpose(1, 0, 2, 3)
    own_queries = own_queries.reshape(req_local, QROWS, HD)
    copies = jnp.broadcast_to(own_queries, (16, req_local, QROWS, HD)).reshape(-1, QROWS, HD)
    every_query = lax.all_to_all(copies, "inst", 0, 0, tiled=True)

    own = jnp.concatenate([k_prefill, v_prefill], axis=1)
    up = permute(own, moves(0, 1, 0))
    down = permute(own, moves(0, -1, 0))
    across = permute(own, moves(1, 0, 0))
    beside = permute(own, moves(0, 0, 1))
    up, down, across = after([up, down, across], [every_query])
    mirror = [(i, 15 - i) for i in range(16)]
    up_more = permute(jnp.concatenate([across, up[:ROWS]]), moves(0, 1, 0))
    down_more = permute(jnp.concatenate([across, down[ROWS:]]), moves(0, -1, 0))
    beside_near = permute(jnp.concatenate([up, down, across]), moves(0, 0, 1))
    block_count, block_len = k_cache.shape[:2]
    width = block_table.shape[1]
    global_id = me * block_count + jnp.arange(block_count, dtype=jnp.int32)
    matches = block_table.reshape(-1)[None, :] == global_id[:, None]
    place = jnp.arange(block_table.size, dtype=jnp.int32)[None, :]
    flat = jnp.sum(jnp.where(matches, place, 0), axis=1)
    owner = flat // width
    left = req_lengths[:, None] - jnp.arange(width, dtype=jnp.int32)[None, :] * block_len
    left = jnp.clip(left, 0, block_len).reshape(-1)
    live = jnp.sum(jnp.where(matches, left[None, :], 0), axis=1)
    every_query = after([every_query], [beside_near])[0]
    parts = decode_cache(owner, live, every_query, k_cache, v_cache)
    received = lax.all_to_all(parts, "inst", 0, 0, tiled=True)

    second_rows = after([q_prefill], [parts])[0][ROWS:]
    other_rows = permute(second_rows, mirror)
    queries = [q_prefill, other_rows]

    up_more, down_more = after([up_more, down_more], [second_rows])
    up_last = permute(up_more[:KEYS], moves(0, 1, 0))
    down_last = permute(down_more[:KEYS], moves(0, -1, 1))
    beside_far = permute(jnp.concatenate([up_more, down_more]), moves(0, 0, 1))

    near_ids = [
        me,
        index_of(z, y, c + 1),
        index_of(z, y + 3, c),
        index_of(z, y + 1, c),
        index_of(z + 1, y, c),
        index_of(z, y + 3, c + 1),
        index_of(z, y + 1, c + 1),
        index_of(z + 1, y, c + 1),
    ]
    far_ids = [
        index_of(z, y + 2, c),
        index_of(z + 1, y + 3, c),
        index_of(z + 1, y + 1, c),
        index_of(z + 1, y + 2, c),
        index_of(z, y + 2, c + 1),
        index_of(z + 1, y + 3, c + 1),
        index_of(z + 1, y + 1, c + 1),
        index_of(z + 1, y + 2, c + 1),
    ]
    near_sources = [(k, 0, KEYS, k, 0) for k in range(5)]
    near_sources += [(5, k * KEYS, KEYS, 5 + k, 0) for k in range(3)]
    mirror_slot = jnp.where(y % 2 == 0, 5, 6)
    numbers = jnp.stack([*near_ids, *far_ids, me, 15 - me, mirror_slot]).astype(jnp.int32)
    own = after([own], [parts])[0]
    state = flash(
        numbers,
        queries,
        [own, beside, up, down, across, beside_near],
        near_sources,
        diag=(0, 0),
        diag_slot=0,
    )

    both = KEYS + ROWS
    far_sources = [
        (0, KEYS, ROWS, 0, 0),
        (1, KEYS, ROWS, 0, ROWS),
        (0, 0, KEYS, 1, 0),
        (1, 0, KEYS, 2, 0),
        (2, 0, KEYS, 3, 0),
        (4, KEYS, ROWS, 4, 0),
        (4, both + KEYS, ROWS, 4, ROWS),
        (4, 0, KEYS, 5, 0),
        (4, both, KEYS, 6, 0),
        (3, 0, KEYS, 7, 0),
    ]
    *state, received = lax.optimization_barrier((*state, received))
    received = received.reshape(-1, req_local, 2 * QROWS, HD)
    decode_out = decode_merge(received, own_queries, k_new, v_new)
    decode_out = decode_out.reshape(req_local, steps, HEADS * HD).transpose(1, 0, 2)

    own_out, other_out = flash(
        numbers,
        queries,
        [up_more, down_more, up_last, down_last, beside_far],
        far_sources,
        state=state,
        final=True,
        diag=(1, ROWS),
    )
    last_rows = permute(other_out, mirror)
    return lax.dynamic_update_slice(own_out, last_rows, (ROWS, 0)), decode_out


def solution(mesh):
    placed = (
        P("inst", "tp"),
        P("inst", "tp"),
        P("inst", "tp"),
        P(None, "inst", "tp"),
        P(None, "inst", "tp"),
        P(None, "inst", "tp"),
        P("inst", None, "tp"),
        P("inst", None, "tp"),
        P(),
        P(),
    )
    return jax.shard_map(
        body,
        mesh=mesh,
        in_specs=placed,
        out_specs=(P("inst", "tp"), P(None, "inst", "tp")),
        check_vma=False,
    )
```
